256 devices in a mesh: ia: 32 (over z, x), ja: 4 (over y), ka: 2 (over core).
Axes of the slice: x: 4, y: 4, z: 8, core: 2. Of those that a mesh axis runs over, the one named last changes fastest.
Arguments:
- tensor: bfloat16 [4, 16384, 16384], P('ka', 'ia', 'ja'), may hold values from -6144 to 6144
- factor_b: bfloat16 [4, 4096, 256], P('ja', ('ia', 'ka')), may hold values from -180 to 180
- factor_c: bfloat16 [2, 2, 256], P('ka'), may hold values from 0.5 to 1.5
Outputs:
- factor_a: float32 [32, 512, 256], P('ia', ('ja', 'ka'))
The draws below stay inside these ranges and needn't reach their ends.
All inputs are finite; a program needn't handle non-finite values.
Results may differ from the reference program's by a relative error of at most 0.0003.
Values may be sent and summed in bfloat16 or wider, within the bound.
A program may use at most 64 MiB of HBM per device.

```python
import math
import jax
import jax.numpy as jnp
from jax import lax

RANK = 256
I_DEV = 512
J_DEV = 4096
K_DEV = 2
IB = 32
JB = 4
KB = 2
NI = 16384
NJ = 16384
NK = 4


def draw_factor_b(key, part):
    key = jax.random.fold_in(key, 11)
    first, second, third = jax.random.split(key, 3)
    shape = (JB, J_DEV, RANK)
    row_scale = jnp.exp(jax.random.uniform(second, (JB, J_DEV, 1), jnp.float32, 0.0, math.log(10.0)))
    col_scale = jnp.exp(jax.random.uniform(third, (1, 1, RANK), jnp.float32, 0.0, math.log(10.0)))
    position = (jnp.arange(JB, dtype=jnp.float32)[:, None] * J_DEV + jnp.arange(J_DEV, dtype=jnp.float32)[None, :]) / (JB * J_DEV)
    trend = jnp.exp(math.log(3.0) * position)[:, :, None]
    values = jnp.clip(jax.random.normal(first, shape, jnp.float32), -6.0, 6.0)
    return (values * row_scale * col_scale * trend / 10.0).astype(jnp.bfloat16)


def level_of(rng, dims, cuts, smallest, top_value):
    gain = 1.0
    for axis_at, shards_of in cuts:
        draws = jax.random.uniform(jax.random.fold_in(jax.random.fold_in(rng, 6), axis_at), (shards_of,), jnp.float32, smallest / len(cuts), top_value / len(cuts))
        gain = gain * jnp.repeat(jnp.exp(draws), dims[axis_at] // shards_of).reshape((-1,) + (1,) * (len(dims) - 1 - axis_at))
    return gain


def gaussian(rng, dims, width, limit, shards=(), kind=jnp.bfloat16):
    level = level_of(rng, dims, shards, -0.22, 0.18) if shards else 1.0
    array = jax.random.normal(rng, dims, jnp.float32) * width * level
    return jnp.minimum(jnp.maximum(array, -limit), limit).astype(kind)


def setup_inputs(seed: int = 0) -> dict:
    streams_of = jax.random.split(jax.random.key(seed), 4)
    tensor = gaussian(streams_of[0], (NK, NI, NJ), (J_DEV // 4), 6144.0, ((0, 2), (1, 32), (2, 4)))
    factor_b = draw_factor_b(jax.random.fold_in(streams_of[3], 71), 0)
    factor_c = jnp.clip(0.5 + 1.0 * jax.random.uniform(streams_of[2], (KB, K_DEV, RANK), jnp.float32) ** level_of(streams_of[2], (KB, K_DEV, RANK), ((0, 2),), -0.2, 0.2), 0.5, 1.5).astype(jnp.bfloat16)
    return {"tensor": tensor, "factor_b": factor_b, "factor_c": factor_c}


def reference(tensor, factor_b, factor_c):
    flat_b = factor_b.reshape(NJ, RANK)
    flat_c = factor_c.reshape(NK, RANK)
    mttkrp = jnp.zeros((NI, RANK), jnp.float32)
    for slab in range(NK):
        product = jnp.dot(tensor[slab].astype(jnp.float32), flat_b.astype(jnp.float32), preferred_element_type=jnp.float32)
        mttkrp = mttkrp + product * flat_c[slab].astype(jnp.float32)[None, :]
    gram_b = jnp.dot(flat_b.T.astype(jnp.float32), flat_b.astype(jnp.float32), preferred_element_type=jnp.float32)
    gram_c = jnp.dot(flat_c.T.astype(jnp.float32), flat_c.astype(jnp.float32), preferred_element_type=jnp.float32)
    lower = jnp.linalg.cholesky(gram_b * gram_c)
    middle = lax.linalg.triangular_solve(lower, mttkrp, left_side=False, lower=True, transpose_a=True)
    result = lax.linalg.triangular_solve(lower, middle, left_side=False, lower=True, transpose_a=False)
    return result.reshape(IB, I_DEV, RANK)
```

```python
import jax, jax.numpy as jnp
from jax import lax
from jax.experimental import pallas as pl
from jax.sharding import PartitionSpec as P
HI=lax.Precision.HIGHEST


def dot(a,b,ta=False,tb=False):
    return lax.dot_general(a,b,(((0 if ta else 1,),(1 if tb else 0,)),((),())),precision=HI,preferred_element_type=jnp.float32)


def gj128(block):
    tiles=[block[8*q:8*q+8,:] for q in range(16)]
    lane=lax.broadcasted_iota(jnp.int32,(8,128),1)
    sub=lax.broadcasted_iota(jnp.int32,(8,128),0)
    lb=lambda v,k: jnp.broadcast_to(v[:,k:k+1],(8,128))
    sb=lambda v,i: jnp.broadcast_to(v[i:i+1,:],(8,128))
    for p in range(16):
        cols=[lb(tiles[p],8*p+m) for m in range(8)]
        for s in range(4):
            i0,i1=2*s,2*s+1
            k0,k1=8*p+i0,8*p+i1
            c0,c1=cols[i0],cols[i1]
            a,b,d=sb(c0,i0),sb(c1,i0),sb(c1,i1)
            r=1.0/(a*d-b*b)
            at0,at1=lane==k0,lane==k1
            either=at0|at1
            rows=(sub==i0)|(sub==i1)
            e0=jnp.where(sub==i0,-1.0,jnp.where(sub==i1,0.0,c0))
            e1=jnp.where(sub==i1,-1.0,jnp.where(sub==i0,0.0,c1))
            T=tiles[p]
            row0,row1=sb(T,i0),sb(T,i1)
            w0=jnp.where(at0,-d,jnp.where(at1,b,d*row0-b*row1))*r
            w1=jnp.where(at0,b,jnp.where(at1,-a,a*row1-b*row0))*r
            for m in range(i1+1,8):
                t0,t1=sb(cols[m],i0),sb(cols[m],i1)
                g=e0*(d*t0-b*t1)+e1*(a*t1-b*t0)
                cols[m]=jnp.where(rows,0.0,cols[m])-g*r
            new=[]
            for q in range(16):
                t=tiles[q]
                if q==p:
                    new.append(jnp.where(either|rows,0.0,t)-e0*w0-e1*w1)
                else:
                    new.append(jnp.where(either,0.0,t)-lb(t,k0)*w0-lb(t,k1)*w1)
            tiles=new
    return -jnp.concatenate(tiles,axis=0)


def solve_kernel(gb_ref,c_ref,m_ref,o_ref):
    c=c_ref[...]
    gc=lax.dot_general(c,c,(((0,),(0,)),((),())),preferred_element_type=jnp.float32)
    n=gb_ref[...]*gc
    eye=lax.broadcasted_iota(jnp.int32,n.shape,0)==lax.broadcasted_iota(jnp.int32,n.shape,1)
    diag=jnp.where(eye,n,0.0)
    sr=lax.rsqrt(jnp.sum(diag,axis=0,keepdims=True))
    sc=lax.rsqrt(jnp.sum(diag,axis=1,keepdims=True))
    n=n*sr*sc
    m=m_ref[...]*sr
    n11,n12,n22=n[:128,:128],n[:128,128:],n[128:,128:]
    m1,m2=m[:,:128],m[:,128:]
    i1=gj128(n11)
    t=dot(i1,n12)
    i2=gj128(n22-dot(n12,t,ta=True))
    z=dot(m2-dot(m1,t),i2)
    a1=dot(m1,i1)-dot(z,t,tb=True)
    o_ref[...]=jnp.concatenate([a1,z],axis=1)*sr


def per_device(tensor, factor_b, factor_c):
    block = lax.all_gather(factor_b, ("ia", "ka"), axis=1, tiled=True)[0]
    gram = lax.dot_general(
        block, block, (((0,), (0,)), ((), ())), preferred_element_type=jnp.float32
    )
    gram = lax.psum(gram, "ja")
    c_all = lax.all_gather(factor_c[0], "ka", axis=0, tiled=True)
    slabs = jnp.einsum("kin,nr->kir", tensor, block, preferred_element_type=jnp.float32)
    mttkrp = jnp.sum(slabs * factor_c[0].astype(jnp.float32)[:, None, :], axis=0)
    rows = lax.psum_scatter(mttkrp, ("ja", "ka"), scatter_dimension=0, tiled=True)
    out = pl.pallas_call(
        solve_kernel, out_shape=jax.ShapeDtypeStruct(rows.shape, jnp.float32), name="solve"
    )(gram, c_all, rows)
    return out[None]


def solution(mesh):
    return jax.shard_map(
        per_device,
        mesh=mesh,
        in_specs=(P("ka", "ia", "ja"), P("ja", ("ia", "ka"), None), P("ka", None, None)),
        out_specs=P("ia", ("ja", "ka"), None),
        check_vma=False,
    )
```

```python
import jax, jax.numpy as jnp
from jax import lax
from jax.experimental import pallas as pl
from jax.experimental.pallas import tpu as pltpu
from jax.sharding import PartitionSpec as P
HI=lax.Precision.HIGHEST


def dot(a,b,ta=False,tb=False):
    return lax.dot_general(a,b,(((0 if ta else 1,),(1 if tb else 0,)),((),())),precision=HI,preferred_element_type=jnp.float32)


def gj128(block):
    tiles=[block[8*q:8*q+8,:] for q in range(16)]
    lane=lax.broadcasted_iota(jnp.int32,(8,128),1)
    sub=lax.broadcasted_iota(jnp.int32,(8,128),0)
    lb=lambda v,k: jnp.broadcast_to(v[:,k:k+1],(8,128))
    sb=lambda v,i: jnp.broadcast_to(v[i:i+1,:],(8,128))
    for p in range(16):
        cols=[lb(tiles[p],8*p+m) for m in range(8)]
        for s in range(4):
            i0,i1=2*s,2*s+1
            k0,k1=8*p+i0,8*p+i1
            c0,c1=cols[i0],cols[i1]
            a,b,d=sb(c0,i0),sb(c1,i0),sb(c1,i1)
            r=1.0/(a*d-b*b)
            at0,at1=lane==k0,lane==k1
            either=at0|at1
            rows=(sub==i0)|(sub==i1)
            e0=jnp.where(sub==i0,-1.0,jnp.where(sub==i1,0.0,c0))
            e1=jnp.where(sub==i1,-1.0,jnp.where(sub==i0,0.0,c1))
            T=tiles[p]
            row0,row1=sb(T,i0),sb(T,i1)
            w0=jnp.where(at0,-d,jnp.where(at1,b,d*row0-b*row1))*r
            w1=jnp.where(at0,b,jnp.where(at1,-a,a*row1-b*row0))*r
            for m in range(i1+1,8):
                t0,t1=sb(cols[m],i0),sb(cols[m],i1)
                g=e0*(d*t0-b*t1)+e1*(a*t1-b*t0)
                cols[m]=jnp.where(rows,0.0,cols[m])-g*r
            new=[]
            for q in range(16):
                t=tiles[q]
                if q==p:
                    new.append(jnp.where(either|rows,0.0,t)-e0*w0-e1*w1)
                else:
                    new.append(jnp.where(either,0.0,t)-lb(t,k0)*w0-lb(t,k1)*w1)
            tiles=new
    return -jnp.concatenate(tiles,axis=0)


def solve_kernel(gb_ref,c_ref,m_ref,o_ref):
    c=c_ref[...].astype(jnp.bfloat16)
    gc=lax.dot_general(c,c,(((0,),(0,)),((),())),preferred_element_type=jnp.float32)
    n=gb_ref[...]*gc
    eye=lax.broadcasted_iota(jnp.int32,n.shape,0)==lax.broadcasted_iota(jnp.int32,n.shape,1)
    diag=jnp.where(eye,n,0.0)
    sr=lax.rsqrt(jnp.sum(diag,axis=0,keepdims=True))
    sc=lax.rsqrt(jnp.sum(diag,axis=1,keepdims=True))
    n=n*sr*sc
    m=m_ref[...]*sr
    n11,n12,n22=n[:128,:128],n[:128,128:],n[128:,128:]
    m1,m2=m[:,:128],m[:,128:]
    i1=gj128(n11)
    t=dot(i1,n12)
    i2=gj128(n22-dot(n12,t,ta=True))
    z=dot(m2-dot(m1,t),i2)
    a1=dot(m1,i1)-dot(z,t,tb=True)
    o_ref[...]=jnp.concatenate([a1,z],axis=1)*sr


Z, X, Y, CORES = 8, 4, 4, 2
PIECE = 64
RANK = 256
MESH = pl.DeviceIdType.MESH


def distance(step):
    return lax.rem(step, 2) * ((step + 1) // 2) + (1 - lax.rem(step, 2)) * lax.rem(Z - step // 2, Z)


def gather_kernel(
    x_hbm, b_ref, c_ref,
    gram_out, c_out, m_out,
    xbuf, bbuf, acc, gacc, grecv, gsum, gall, cbuf, comb, ccore, csum, crecv_y,
    x_sem, z_send, z_recv, g_send, g_recv, k_send, k_recv, c_send, c_recv,
    gs_send, gs_recv, ga_send, ga_recv, mc_send, mc_recv, my_send, my_recv,
):
    ia, y, c = lax.axis_index("ia"), lax.axis_index("ja"), lax.axis_index("ka")
    z, x = ia // X, lax.rem(ia, X)
    peer = (ia, y, 1 - c)

    def at(dz=0, dx=0, dy=0, core=None):
        zz, xx = lax.rem(z + dz, Z), lax.rem(x + dx, X)
        return (zz * X + xx, lax.rem(y + dy, Y), c if core is None else core)

    def send(src, dst, ss, rs, to):
        copy = pltpu.make_async_remote_copy(
            src_ref=src, dst_ref=dst, send_sem=ss, recv_sem=rs, device_id=to, device_id_type=MESH
        )
        copy.start()

    def arrived(ref, sem):
        pltpu.make_async_remote_copy(
            src_ref=ref, dst_ref=ref, send_sem=sem, recv_sem=sem, device_id=peer, device_id_type=MESH
        ).wait_recv()

    def load(step):
        zz = lax.rem(z + distance(step), Z)
        return pltpu.make_async_copy(
            x_hbm.at[:, :, pl.ds(pl.multiple_of(zz * 512, 512), 512)], xbuf.at[zz], x_sem.at[step]
        )

    partners = [at(dz=d) for d in range(1, Z)] + [at(dx=d) for d in range(1, X)]
    partners += [at(dy=d) for d in range(1, Y)] + [at(dy=d, core=1 - c) for d in range(1, Y)] + [peer]
    barrier = pltpu.get_barrier_semaphore()
    for to in partners:
        pl.semaphore_signal(barrier, inc=1, device_id=to, device_id_type=MESH)
    for step in range(Z):
        load(jnp.int32(step)).start()
    bbuf[z, x, c] = b_ref[0]
    cbuf[c] = jnp.concatenate([c_ref[0].astype(jnp.float32), jnp.zeros((6, RANK), jnp.float32)], axis=0)
    acc[...] = jnp.zeros_like(acc)
    gacc[...] = jnp.zeros_like(gacc)
    pl.semaphore_wait(barrier, len(partners))

    own = bbuf.at[z, x, c]
    for dx in (1, 3):
        send(own, own, g_send.at[0], g_recv.at[0], at(dx=dx))
    for dz in (1, 7):
        send(own, own, z_send, z_recv.at[Z - dz], at(dz=dz))
    send(own, own, g_send.at[0], g_recv.at[0], at(dx=2))
    for dz in (2, 6, 3, 5, 4):
        send(own, own, z_send, z_recv.at[Z - dz], at(dz=dz))
    send(cbuf.at[c], cbuf.at[c], c_send, c_recv, peer)

    def group(dz):
        return bbuf.at[lax.rem(z + dz, Z), 0:3, c]

    def relay(step, _):
        dz = distance(step)
        zz = lax.rem(z + dz, Z)
        piece = bbuf.at[zz, x, c]
        arrived(piece, z_recv.at[dz])
        send(piece, piece, g_send.at[dz], g_recv.at[dz], at(dx=1))
        send(piece, piece, g_send.at[dz], g_recv.at[dz], at(dx=3))
        half = bbuf.at[zz, x, c, 0:32]
        send(half, half, g_send.at[dz], g_recv.at[dz], at(dx=2))
        return 0

    def to_peer(dz):
        part = bbuf.at[lax.rem(z + dz, Z), :, c]
        send(part, part, k_send, k_recv.at[dz], peer)

    lax.fori_loop(1, 3, relay, 0)
    arrived(group(0), g_recv.at[0])
    half = bbuf.at[z, lax.rem(x + 2, X), c, 32:64]
    for dz in (1, 7, 2, 6, 3, 5, 4):
        send(half, half, g_send.at[dz], g_recv.at[Z - dz], at(dz=dz))
    to_peer(0)
    lax.fori_loop(3, Z, relay, 0)

    def own_group(step):
        dz = distance(step)
        arrived(group(dz), g_recv.at[dz])
        to_peer(dz)

    def gram_part(step):
        dz = distance(step)
        zz = lax.rem(z + dz, Z)
        arrived(bbuf.at[zz, :, 1 - c], k_recv.at[dz])
        block = bbuf[zz].reshape(512, RANK)
        mine = bbuf[zz, :, :, :, pl.ds(pl.multiple_of(c * 128, 128), 128)].reshape(512, 128)
        gacc[...] += lax.dot_general(
            mine, block, (((0,), (0,)), ((), ())), preferred_element_type=jnp.float32
        ).reshape(Y, 32, RANK)

    def product(step):
        zz = lax.rem(z + distance(step), Z)
        load(step).wait()
        block = bbuf[zz].reshape(512, RANK)
        acc[...] += jnp.dot(
            xbuf[zz].reshape(1024, 512), block, preferred_element_type=jnp.float32
        )

    def chunk(step, _):
        own_group(step + 1)
        gram_part(step)
        product(step)
        return 0

    lax.fori_loop(0, Z - 1, chunk, 0)
    gram_part(jnp.int32(Z - 1))
    for dy in (1, 3, 2):
        send(gacc.at[lax.rem(y + dy, Y)], grecv.at[Y - dy - 1], gs_send, gs_recv.at[Y - dy - 1], at(dy=dy))
    product(jnp.int32(Z - 1))
    rows = c_ref[0].astype(jnp.float32)
    mixed = acc[0:512] * rows[0:1] + acc[512:1024] * rows[1:2]
    comb[...] = mixed.reshape(Y, CORES, PIECE, RANK)
    send(comb.at[:, 1 - c], ccore, mc_send, mc_recv, peer)

    for d in range(3):
        arrived(grecv.at[d], gs_recv.at[d])
    gsum[...] = gacc[y] + grecv[0] + grecv[1] + grecv[2]
    for dy in (1, 3, 2):
        for core in (c, 1 - c):
            send(gsum, gall.at[c * Y + y], ga_send, ga_recv, at(dy=dy, core=core))
    send(gsum, gall.at[c * Y + y], ga_send, ga_recv, peer)

    arrived(ccore, mc_recv)
    csum[...] = ccore[...] + comb[:, c]
    for dy in (1, 3, 2):
        send(csum.at[lax.rem(y + dy, Y)], crecv_y.at[Y - dy - 1], my_send, my_recv.at[Y - dy - 1], at(dy=dy))
    arrived(cbuf.at[1 - c], c_recv)
    c_out[...] = cbuf[...].reshape(16, RANK)
    arrived(gall.at[0:7], ga_recv)
    gall[c * Y + y] = gsum[...]
    gram_out[...] = gall[...].reshape(RANK, RANK)
    for d in range(3):
        arrived(crecv_y.at[d], my_recv.at[d])
    m_out[...] = csum[y] + crecv_y[0] + crecv_y[1] + crecv_y[2]

    def sent(ref, sem):
        pltpu.make_async_remote_copy(
            src_ref=ref, dst_ref=ref, send_sem=sem, recv_sem=sem, device_id=peer, device_id_type=MESH
        ).wait_send()

    sent(bbuf.at[0:7, 0, c], z_send)
    for dz in range(Z):
        sent(group(dz), g_send.at[dz])
    sent(bbuf.at[:, :, c], k_send)
    sent(cbuf.at[c], c_send)
    sent(grecv, gs_send)
    sent(gall.at[0:7], ga_send)
    sent(ccore, mc_send)
    sent(crecv_y, my_send)


def per_device(tensor, factor_b, factor_c):
    f32, bf16 = jnp.float32, jnp.bfloat16
    vmem = pl.BlockSpec(memory_space=pltpu.VMEM)
    dma = pltpu.SemaphoreType.DMA
    gram, c_all, rows = pl.pallas_call(
        gather_kernel,
        out_shape=(
            jax.ShapeDtypeStruct((RANK, RANK), f32),
            jax.ShapeDtypeStruct((16, RANK), f32),
            jax.ShapeDtypeStruct((PIECE, RANK), f32),
        ),
        in_specs=[pl.BlockSpec(memory_space=pl.ANY), vmem, vmem],
        out_specs=(vmem, vmem, vmem),
        scratch_shapes=[
            pltpu.VMEM((Z, 2, 512, 512), bf16),
            pltpu.VMEM((Z, X, CORES, PIECE, RANK), bf16),
            pltpu.VMEM((1024, RANK), f32),
            pltpu.VMEM((Y, 32, RANK), f32),
            pltpu.VMEM((3, 32, RANK), f32),
            pltpu.VMEM((32, RANK), f32),
            pltpu.VMEM((8, 32, RANK), f32),
            pltpu.VMEM((CORES, 8, RANK), f32),
            pltpu.VMEM((Y, CORES, PIECE, RANK), f32),
            pltpu.VMEM((Y, PIECE, RANK), f32),
            pltpu.VMEM((Y, PIECE, RANK), f32),
            pltpu.VMEM((3, PIECE, RANK), f32),
            dma((Z,)), dma, dma((Z,)), dma((Z,)), dma((Z,)), dma, dma((Z,)), dma, dma,
            dma, dma((3,)), dma, dma, dma, dma, dma, dma((3,)),
        ],
        compiler_params=pltpu.CompilerParams(
            collective_id=0, has_side_effects=True, vmem_limit_bytes=48 * 2**20
        ),
        cost_estimate=pl.CostEstimate(flops=2**31, bytes_accessed=2**23, transcendentals=0),
        name="contract",
    )(tensor, factor_b, factor_c)
    out = pl.pallas_call(
        solve_kernel, out_shape=jax.ShapeDtypeStruct(rows.shape, f32), name="solve"
    )(gram, c_all, rows)
    return out[None]


def solution(mesh):
    return jax.shard_map(
        per_device,
        mesh=mesh,
        in_specs=(P("ka", "ia", "ja"), P("ja", ("ia", "ka"), None), P("ka", None, None)),
        out_specs=P("ia", ("ja", "ka"), None),
        check_vma=False,
    )
```

```python
import jax, jax.numpy as jnp
from jax import lax
from jax.experimental import pallas as pl
from jax.experimental.pallas import tpu as pltpu
from jax.sharding import PartitionSpec as P
HI=lax.Precision.HIGHEST


def dot(a,b,ta=False,tb=False):
    return lax.dot_general(a,b,(((0 if ta else 1,),(1 if tb else 0,)),((),())),precision=HI,preferred_element_type=jnp.float32)


def gj128(block, hook=None):
    tiles=[block[8*q:8*q+8,:] for q in range(16)]
    lane=lax.broadcasted_iota(jnp.int32,(8,128),1)
    sub=lax.broadcasted_iota(jnp.int32,(8,128),0)
    lb=lambda v,k: jnp.broadcast_to(v[:,k:k+1],(8,128))
    sb=lambda v,i: jnp.broadcast_to(v[i:i+1,:],(8,128))
    for p in range(16):
        if hook is not None:
            hook(p)
        cols=[lb(tiles[p],8*p+m) for m in range(8)]
        for s in range(4):
            i0,i1=2*s,2*s+1
            k0,k1=8*p+i0,8*p+i1
            c0,c1=cols[i0],cols[i1]
            a,b,d=sb(c0,i0),sb(c1,i0),sb(c1,i1)
            r=1.0/(a*d-b*b)
            at0,at1=lane==k0,lane==k1
            either=at0|at1
            rows=(sub==i0)|(sub==i1)
            e0=jnp.where(sub==i0,-1.0,jnp.where(sub==i1,0.0,c0))
            e1=jnp.where(sub==i1,-1.0,jnp.where(sub==i0,0.0,c1))
            T=tiles[p]
            row0,row1=sb(T,i0),sb(T,i1)
            w0=jnp.where(at0,-d,jnp.where(at1,b,d*row0-b*row1))*r
            w1=jnp.where(at0,b,jnp.where(at1,-a,a*row1-b*row0))*r
            for m in range(i1+1,8):
                t0,t1=sb(cols[m],i0),sb(cols[m],i1)
                g=e0*(d*t0-b*t1)+e1*(a*t1-b*t0)
                cols[m]=jnp.where(rows,0.0,cols[m])-g*r
            new=[]
            for q in range(16):
                t=tiles[q]
                if q==p:
                    new.append(jnp.where(either|rows,0.0,t)-e0*w0-e1*w1)
                else:
                    new.append(jnp.where(either,0.0,t)-lb(t,k0)*w0-lb(t,k1)*w1)
            tiles=new
    return -jnp.concatenate(tiles,axis=0)


Z, X, Y, CORES = 8, 4, 4, 2
PIECE = 64
RANK = 256
MESH = pl.DeviceIdType.MESH


def distance(step):
    return lax.rem(step, 2) * ((step + 1) // 2) + (1 - lax.rem(step, 2)) * lax.rem(Z - step // 2, Z)


def als_kernel(
    x_hbm, b_hbm, c_ref, out_ref,
    xbuf, bbuf, acc, cbuf, gpart, gxy, gz, gslice, gall, comb, ccore, csum, my,
    x_sem, b_sem, z_send, z_recv, g_send, g_recv, k_send, k_recv, o_send, o_recv, c_send, c_recv,
    gxy_send, gxy_recv, gz_send, gz_recv, ga_send, ga_recv, gp_send, gp_recv,
    mc_send, mc_recv, my_send, my_recv,
):
    ia, y, c = lax.axis_index("ia"), lax.axis_index("ja"), lax.axis_index("ka")
    z, x = ia // X, lax.rem(ia, X)
    peer = (ia, y, 1 - c)
    slot = y * X + x

    def at(dz=0, dx=0, dy=0):
        zz, xx = lax.rem(z + dz, Z), lax.rem(x + dx, X)
        return (zz * X + xx, lax.rem(y + dy, Y), c)

    def send(src, dst, ss, rs, to):
        copy = pltpu.make_async_remote_copy(
            src_ref=src, dst_ref=dst, send_sem=ss, recv_sem=rs, device_id=to, device_id_type=MESH
        )
        copy.start()

    def arrived(ref, sem):
        pltpu.make_async_remote_copy(
            src_ref=ref, dst_ref=ref, send_sem=sem, recv_sem=sem, device_id=peer, device_id_type=MESH
        ).wait_recv()

    def sent(ref, sem):
        pltpu.make_async_remote_copy(
            src_ref=ref, dst_ref=ref, send_sem=sem, recv_sem=sem, device_id=peer, device_id_type=MESH
        ).wait_send()

    def load(step):
        zz = lax.rem(z + distance(step), Z)
        return pltpu.make_async_copy(
            x_hbm.at[:, :, pl.ds(pl.multiple_of(zz * 512, 512), 512)], xbuf.at[zz], x_sem.at[step]
        )

    plane = [(dx, dy) for dy in (0, 1, 3, 2) for dx in (0, 1, 3, 2) if dx or dy]
    partners = [at(dz=d) for d in range(1, Z)] + [at(dx=dx, dy=dy) for dx, dy in plane] + [peer]
    barrier = pltpu.get_barrier_semaphore()
    for to in partners:
        pl.semaphore_signal(barrier, inc=1, device_id=to, device_id_type=MESH)
    own = bbuf.at[z, x, c]
    own_load = pltpu.make_async_copy(b_hbm.at[0], own, b_sem)
    own_load.start()
    for step in range(Z):
        load(jnp.int32(step)).start()
    cbuf[c] = jnp.concatenate([c_ref[0].astype(jnp.float32), jnp.zeros((6, RANK), jnp.float32)], axis=0)
    acc[...] = jnp.zeros_like(acc)
    own_load.wait()
    pl.semaphore_wait(barrier, len(partners))

    send(own, own, o_send, o_recv, peer)
    for dz in (1, 7, 2, 6, 3, 5, 4):
        send(own, own, z_send, z_recv.at[Z - dz], at(dz=dz))
    send(cbuf.at[c], cbuf.at[c], c_send, c_recv, peer)

    arrived(bbuf.at[z, x, 1 - c], o_recv)
    mine = bbuf[z, x, :, :, pl.ds(pl.multiple_of(c * 128, 128), 128)].reshape(128, 128)
    gpart[...] = lax.dot_general(
        mine, bbuf[z, x].reshape(128, RANK), (((0,), (0,)), ((), ())), preferred_element_type=jnp.float32
    ).reshape(16, 8, RANK)
    for dx, dy in plane:
        target = lax.rem(y + dy, Y) * X + lax.rem(x + dx, X)
        send(gpart.at[target], gxy.at[slot], gxy_send, gxy_recv, at(dx=dx, dy=dy))
    for dx in (1, 3, 2):
        send(own, own, g_send.at[0], g_recv.at[0], at(dx=dx))
    gxy[slot] = gpart[slot]

    def group(dz):
        return bbuf.at[lax.rem(z + dz, Z), 0:3, c]

    def relay(step, _):
        dz = distance(step)
        zz = lax.rem(z + dz, Z)
        piece = bbuf.at[zz, x, c]
        arrived(piece, z_recv.at[dz])
        send(piece, piece, g_send.at[dz], g_recv.at[dz], at(dx=1))
        send(piece, piece, g_send.at[dz], g_recv.at[dz], at(dx=3))
        half = bbuf.at[zz, x, c, 0:32]
        send(half, half, g_send.at[dz], g_recv.at[dz], at(dx=2))
        return 0

    lax.fori_loop(1, 3, relay, 0)
    arrived(group(0), g_recv.at[0])
    half = bbuf.at[z, lax.rem(x + 2, X), c, 32:64]
    for dz in (1, 7, 2, 6, 3, 5, 4):
        send(half, half, g_send.at[dz], g_recv.at[Z - dz], at(dz=dz))
    for dx in (1, 3, 2):
        part = bbuf.at[z, lax.rem(x + dx, X), c]
        send(part, part, o_send, k_recv.at[0], peer)

    arrived(gxy.at[0:15], gxy_recv)
    gz[z] = jnp.sum(gxy[...], axis=0)
    for dz in (4, 3, 5, 2, 6, 1, 7):
        send(gz.at[z], gz.at[z], gz_send, gz_recv, at(dz=dz))
    lax.fori_loop(3, Z, relay, 0)

    def gram_over_plane():
        arrived(gz.at[0:7], gz_recv)
        gslice[...] = jnp.sum(gz[...], axis=0)
        for dx, dy in plane:
            send(gslice, gall.at[c, slot], ga_send, ga_recv, at(dx=dx, dy=dy))
        gall[c, slot] = gslice[...]

    def gram_to_peer():
        arrived(gall.at[c, 0:15], ga_recv)
        send(gall.at[c], gall.at[c], gp_send, gp_recv, peer)

    def chunk(step, _):
        dz = distance(step)
        zz = lax.rem(z + dz, Z)

        @pl.when(step < Z - 1)
        def _():
            later = distance(step + 1)
            arrived(group(later), g_recv.at[later])
            part = bbuf.at[lax.rem(z + later, Z), :, c]
            send(part, part, k_send, k_recv.at[later], peer)

        @pl.when(step == 1)
        def _():
            gram_over_plane()

        @pl.when(step == 5)
        def _():
            gram_to_peer()

        @pl.when(step == 0)
        def _():
            arrived(bbuf.at[z, 0:3, 1 - c], k_recv.at[0])

        @pl.when(step > 0)
        def _():
            arrived(bbuf.at[zz, :, 1 - c], k_recv.at[dz])

        load(step).wait()
        acc[...] += jnp.dot(
            xbuf[zz].reshape(1024, 512), bbuf[zz].reshape(512, RANK), preferred_element_type=jnp.float32
        )
        return 0

    lax.fori_loop(0, Z, chunk, 0)
    rows = c_ref[0].astype(jnp.float32)
    mixed = acc[0:512] * rows[0:1] + acc[512:1024] * rows[1:2]
    comb[...] = mixed.reshape(Y, CORES, PIECE, RANK)
    send(comb.at[:, 1 - c], ccore, mc_send, mc_recv, peer)

    arrived(cbuf.at[1 - c], c_recv)
    arrived(gall.at[1 - c], gp_recv)
    factor = cbuf[...].reshape(16, RANK).astype(jnp.bfloat16)
    n = gall[...].reshape(RANK, RANK) * lax.dot_general(
        factor, factor, (((0,), (0,)), ((), ())), preferred_element_type=jnp.float32
    )
    eye = lax.broadcasted_iota(jnp.int32, n.shape, 0) == lax.broadcasted_iota(jnp.int32, n.shape, 1)
    diag = jnp.where(eye, n, 0.0)
    sr = lax.rsqrt(jnp.sum(diag, axis=0, keepdims=True))
    sc = lax.rsqrt(jnp.sum(diag, axis=1, keepdims=True))
    n = n * sr * sc
    n11, n12, n22 = n[:128, :128], n[:128, 128:], n[128:, 128:]

    def hook(p):
        if p != 4:
            return
        arrived(ccore, mc_recv)
        csum[...] = ccore[...] + comb[:, c]
        for dy in (1, 3, 2):
            send(csum.at[lax.rem(y + dy, Y)], my.at[y], my_send, my_recv, at(dy=dy))
        my[y] = csum[y]

    i1 = gj128(n11, hook)
    t = dot(i1, n12)
    i2 = gj128(n22 - dot(n12, t, ta=True))
    arrived(my.at[0:3], my_recv)
    m = jnp.sum(my[...], axis=0) * sr
    m1, m2 = m[:, :128], m[:, 128:]
    last = dot(m2 - dot(m1, t), i2)
    first = dot(m1, i1) - dot(last, t, tb=True)
    out_ref[0] = jnp.concatenate([first, last], axis=1) * sr

    sent(bbuf.at[z, :, c], o_send)
    sent(bbuf.at[0:7, 0, c], z_send)
    for dz in range(Z):
        sent(group(dz), g_send.at[dz])
    sent(bbuf.at[0:7, :, c], k_send)
    sent(cbuf.at[c], c_send)
    sent(gxy.at[0:15], gxy_send)
    sent(gz.at[0:7], gz_send)
    sent(gxy.at[0:15], ga_send)
    sent(gall.at[c], gp_send)
    sent(ccore, mc_send)
    sent(my.at[0:3], my_send)


def per_device(tensor, factor_b, factor_c):
    f32, bf16 = jnp.float32, jnp.bfloat16
    vmem = pl.BlockSpec(memory_space=pltpu.VMEM)
    hbm = pl.BlockSpec(memory_space=pl.ANY)
    dma = pltpu.SemaphoreType.DMA
    return pl.pallas_call(
        als_kernel,
        out_shape=jax.ShapeDtypeStruct((1, PIECE, RANK), f32),
        in_specs=[hbm, hbm, vmem],
        out_specs=vmem,
        scratch_shapes=[
            pltpu.VMEM((Z, 2, 512, 512), bf16),
            pltpu.VMEM((Z, X, CORES, PIECE, RANK), bf16),
            pltpu.VMEM((1024, RANK), f32),
            pltpu.VMEM((CORES, 8, RANK), f32),
            pltpu.VMEM((16, 8, RANK), f32),
            pltpu.VMEM((16, 8, RANK), f32),
            pltpu.VMEM((Z, 8, RANK), f32),
            pltpu.VMEM((8, RANK), f32),
            pltpu.VMEM((CORES, 16, 8, RANK), f32),
            pltpu.VMEM((Y, CORES, PIECE, RANK), f32),
            pltpu.VMEM((Y, PIECE, RANK), f32),
            pltpu.VMEM((Y, PIECE, RANK), f32),
            pltpu.VMEM((Y, PIECE, RANK), f32),
            dma((Z,)), dma, dma, dma((Z,)), dma((Z,)), dma((Z,)), dma, dma((Z,)), dma, dma, dma, dma,
            dma, dma, dma, dma, dma, dma, dma, dma, dma, dma, dma, dma,
        ],
        compiler_params=pltpu.CompilerParams(
            collective_id=0, has_side_effects=True, vmem_limit_bytes=48 * 2**20
        ),
        cost_estimate=pl.CostEstimate(flops=2**31, bytes_accessed=2**23, transcendentals=0),
        name="als",
    )(tensor, factor_b, factor_c)


def solution(mesh):
    return jax.shard_map(
        per_device,
        mesh=mesh,
        in_specs=(P("ka", "ia", "ja"), P("ja", ("ia", "ka"), None), P("ka", None, None)),
        out_specs=P("ia", ("ja", "ka"), None),
        check_vma=False,
    )
```

```python
import jax, jax.numpy as jnp
from jax import lax
from jax.experimental import pallas as pl
from jax.experimental.pallas import tpu as pltpu
from jax.sharding import PartitionSpec as P
HI=lax.Precision.HIGHEST


def dot(a,b,ta=False,tb=False):
    return lax.dot_general(a,b,(((0 if ta else 1,),(1 if tb else 0,)),((),())),precision=HI,preferred_element_type=jnp.float32)


def split(v):
    hi = v.astype(jnp.bfloat16)
    rest = v - hi.astype(jnp.float32)
    mid = rest.astype(jnp.bfloat16)
    return hi, mid, (rest - mid.astype(jnp.float32)).astype(jnp.bfloat16)


def invert(aref, hook=None):
    lane = lax.broadcasted_iota(jnp.int32, (8, 128), 1)
    sub = lax.broadcasted_iota(jnp.int32, (8, 128), 0)

    def read(row):
        return [aref[row : row + 8, 0:128], aref[row : row + 8, 128:256]]

    def over_lanes(tile, k):
        v = tile[k // 128]
        return jnp.broadcast_to(v[:, k % 128 : k % 128 + 1], (8, 128))

    def over_rows(v, i):
        return jnp.broadcast_to(v[i : i + 1, :], (8, 128))

    def eliminate(tile, first, done):
        count = 8 * len(done)
        half, off = first // 128, first % 128
        spread = [over_lanes(tile, first + m) for m in range(count)]
        new = []
        for side in range(2):
            parts = [spread[m] * over_rows(done[m // 8][side], m % 8) for m in range(count)]
            while len(parts) > 1:
                parts = [parts[i] + parts[i + 1] for i in range(0, len(parts), 2)]
            kept = tile[side]
            if side == half:
                kept = jnp.where((lane >= off) & (lane < off + count), 0.0, kept)
            new.append(kept - parts[0])
        return new

    tiles = [read(0), read(8)]
    for panel in range(16):
        if hook is not None:
            hook(panel)
        base = 16 * panel
        half, off = base // 128, base % 128
        for h in range(2):
            cols = [over_lanes(tiles[h], base + 8 * h + m) for m in range(8)]
            for s in range(4):
                i0, i1 = 2 * s, 2 * s + 1
                k0, k1 = base + 8 * h + i0, base + 8 * h + i1
                c0, c1 = cols[i0], cols[i1]
                a, b, d = over_rows(c0, i0), over_rows(c1, i0), over_rows(c1, i1)
                r = 1.0 / (a * d - b * b)
                at0, at1 = lane == k0 % 128, lane == k1 % 128
                either = at0 | at1
                rows = (sub == i0) | (sub == i1)
                e0 = jnp.where(sub == i0, -1.0, jnp.where(sub == i1, 0.0, c0))
                e1 = jnp.where(sub == i1, -1.0, jnp.where(sub == i0, 0.0, c1))
                for m in range(i1 + 1, 8):
                    t0, t1 = over_rows(cols[m], i0), over_rows(cols[m], i1)
                    g = e0 * (d * t0 - b * t1) + e1 * (a * t1 - b * t0)
                    cols[m] = jnp.where(rows, 0.0, cols[m]) - g * r
                mine = []
                for side in range(2):
                    T = tiles[h][side]
                    row0, row1 = over_rows(T, i0), over_rows(T, i1)
                    w0, w1 = d * row0 - b * row1, a * row1 - b * row0
                    T = jnp.where(rows, 0.0, T)
                    if side == half:
                        w0 = jnp.where(at0, -d, jnp.where(at1, b, w0))
                        w1 = jnp.where(at0, b, jnp.where(at1, -a, w1))
                        T = jnp.where(either, 0.0, T)
                    w0, w1 = w0 * r, w1 * r
                    mine.append(T - e0 * w0 - e1 * w1)
                tiles[h] = mine
            tiles[1 - h] = eliminate(tiles[1 - h], base + 8 * h, [tiles[h]])
        done = tiles
        if panel < 15:
            tiles = [eliminate(read(base + 16 + 8 * q), base, done) for q in range(2)]
        w = jnp.concatenate([jnp.concatenate(t, axis=1) for t in done], axis=0)
        wh, wm, wl = split(w)

        def pad(v):
            parts = [v]
            if off:
                parts.insert(0, jnp.zeros((off, 256), jnp.bfloat16))
            if off < 112:
                parts.append(jnp.zeros((112 - off, 256), jnp.bfloat16))
            return jnp.concatenate(parts, axis=0) if len(parts) > 1 else v

        hi, mid, lo = split(aref[:, 128 * half : 128 * half + 128])
        both = jnp.concatenate([hi, mid], axis=1)
        f = lambda l, r0, r1: jnp.dot(l, jnp.concatenate([pad(r0), pad(r1)], axis=0), preferred_element_type=jnp.float32)
        change = f(both, wh, wh) + f(both, wm, wm) + f(jnp.concatenate([hi, lo], axis=1), wl, wh)
        lanes = lax.broadcasted_iota(jnp.int32, (256, 256), 1)
        keep = jnp.where((lanes >= base) & (lanes < base + 16), 0.0, aref[...])
        aref[...] = keep - change
        aref[base : base + 16, :] = w


Z, X, Y, CORES = 8, 4, 4, 2
PIECE = 64
RANK = 256
MESH = pl.DeviceIdType.MESH


def distance(step):
    return lax.rem(step, 2) * ((step + 1) // 2) + (1 - lax.rem(step, 2)) * lax.rem(Z - step // 2, Z)


def als_kernel(
    x_hbm, b_hbm, c_ref, out_ref,
    xbuf, bbuf, acc, cbuf, gpart, gxy, gz, gslice, gall, comb, ccore, csum, my, matrix,
    x_sem, b_sem, z_send, z_recv, g_send, g_recv, k_send, k_recv, o_send, o_recv, c_send, c_recv,
    gxy_send, gxy_recv, gz_send, gz_recv, ga_send, ga_recv, gp_send, gp_recv,
    mc_send, mc_recv, my_send, my_recv,
):
    ia, y, c = lax.axis_index("ia"), lax.axis_index("ja"), lax.axis_index("ka")
    z, x = ia // X, lax.rem(ia, X)
    peer = (ia, y, 1 - c)
    slot = y * X + x

    def at(dz=0, dx=0, dy=0):
        zz, xx = lax.rem(z + dz, Z), lax.rem(x + dx, X)
        return (zz * X + xx, lax.rem(y + dy, Y), c)

    def send(src, dst, ss, rs, to):
        copy = pltpu.make_async_remote_copy(
            src_ref=src, dst_ref=dst, send_sem=ss, recv_sem=rs, device_id=to, device_id_type=MESH
        )
        copy.start()

    def arrived(ref, sem):
        pltpu.make_async_remote_copy(
            src_ref=ref, dst_ref=ref, send_sem=sem, recv_sem=sem, device_id=peer, device_id_type=MESH
        ).wait_recv()

    def sent(ref, sem):
        pltpu.make_async_remote_copy(
            src_ref=ref, dst_ref=ref, send_sem=sem, recv_sem=sem, device_id=peer, device_id_type=MESH
        ).wait_send()

    def load(step):
        zz = lax.rem(z + distance(step), Z)
        return pltpu.make_async_copy(
            x_hbm.at[:, :, pl.ds(pl.multiple_of(zz * 512, 512), 512)], xbuf.at[zz], x_sem.at[step]
        )

    plane = [(dx, dy) for dy in (2, 1, 3, 0) for dx in (2, 1, 3, 0) if dx or dy]
    partners = [at(dz=d) for d in range(1, Z)] + [at(dx=dx, dy=dy) for dx, dy in plane] + [peer]
    barrier = pltpu.get_barrier_semaphore()
    for to in partners:
        pl.semaphore_signal(barrier, inc=1, device_id=to, device_id_type=MESH)
    own = bbuf.at[z, x, c]
    own_load = pltpu.make_async_copy(b_hbm.at[0], own, b_sem)
    own_load.start()
    for step in range(Z):
        load(jnp.int32(step)).start()
    cbuf[c] = jnp.concatenate([c_ref[0].astype(jnp.float32), jnp.zeros((6, RANK), jnp.float32)], axis=0)
    acc[...] = jnp.zeros_like(acc)
    own_load.wait()
    pl.semaphore_wait(barrier, len(partners))

    send(own, own, o_send, o_recv, peer)
    for dz in (1, 7, 2, 6, 3, 5, 4):
        send(own, own, z_send, z_recv.at[Z - dz], at(dz=dz))
    send(cbuf.at[c], cbuf.at[c], c_send, c_recv, peer)

    arrived(bbuf.at[z, x, 1 - c], o_recv)
    mine = bbuf[z, x, :, :, pl.ds(pl.multiple_of(c * 128, 128), 128)].reshape(128, 128)
    gpart[...] = lax.dot_general(
        mine, bbuf[z, x].reshape(128, RANK), (((0,), (0,)), ((), ())), preferred_element_type=jnp.float32
    ).reshape(16, 8, RANK)
    for dx, dy in plane:
        target = lax.rem(y + dy, Y) * X + lax.rem(x + dx, X)
        send(gpart.at[target], gxy.at[slot], gxy_send, gxy_recv, at(dx=dx, dy=dy))
    for dx in (1, 3, 2):
        send(own, own, g_send.at[0], g_recv.at[0], at(dx=dx))
    gxy[slot] = gpart[slot]

    def group(dz):
        return bbuf.at[lax.rem(z + dz, Z), 0:3, c]

    def relay(step, _):
        dz = distance(step)
        zz = lax.rem(z + dz, Z)
        piece = bbuf.at[zz, x, c]
        arrived(piece, z_recv.at[dz])
        send(piece, piece, g_send.at[dz], g_recv.at[dz], at(dx=1))
        send(piece, piece, g_send.at[dz], g_recv.at[dz], at(dx=3))
        half = bbuf.at[zz, x, c, 0:32]
        send(half, half, g_send.at[dz], g_recv.at[dz], at(dx=2))
        return 0

    lax.fori_loop(1, 3, relay, 0)
    arrived(group(0), g_recv.at[0])
    half = bbuf.at[z, lax.rem(x + 2, X), c, 32:64]
    for dz in (1, 7, 2, 6, 3, 5, 4):
        send(half, half, g_send.at[dz], g_recv.at[Z - dz], at(dz=dz))
    for dx in (1, 3, 2):
        part = bbuf.at[z, lax.rem(x + dx, X), c]
        send(part, part, o_send, k_recv.at[0], peer)

    arrived(gxy.at[0:15], gxy_recv)
    gz[z] = jnp.sum(gxy[...], axis=0)
    for dz in (4, 3, 5, 2, 6, 1, 7):
        send(gz.at[z], gz.at[z], gz_send, gz_recv, at(dz=dz))
    lax.fori_loop(3, Z, relay, 0)

    def gram_over_plane():
        arrived(gz.at[0:7], gz_recv)
        gslice[...] = jnp.sum(gz[...], axis=0)
        for dx, dy in plane:
            send(gslice, gall.at[c, slot], ga_send, ga_recv, at(dx=dx, dy=dy))
        gall[c, slot] = gslice[...]

    def gram_to_peer():
        arrived(gall.at[c, 0:15], ga_recv)
        send(gall.at[c], gall.at[c], gp_send, gp_recv, peer)

    def chunk(step, _):
        dz = distance(step)
        zz = lax.rem(z + dz, Z)

        @pl.when(step < Z - 1)
        def _():
            later = distance(step + 1)
            arrived(group(later), g_recv.at[later])
            part = bbuf.at[lax.rem(z + later, Z), :, c]
            send(part, part, k_send, k_recv.at[later], peer)

        @pl.when(step == 1)
        def _():
            gram_over_plane()

        @pl.when(step == 5)
        def _():
            gram_to_peer()

        @pl.when(step == 0)
        def _():
            arrived(bbuf.at[z, 0:3, 1 - c], k_recv.at[0])

        @pl.when(step > 0)
        def _():
            arrived(bbuf.at[zz, :, 1 - c], k_recv.at[dz])

        load(step).wait()
        acc[...] += jnp.dot(
            xbuf[zz].reshape(1024, 512), bbuf[zz].reshape(512, RANK), preferred_element_type=jnp.float32
        )
        return 0

    lax.fori_loop(0, Z, chunk, 0)
    rows = c_ref[0].astype(jnp.float32)
    mixed = acc[0:512] * rows[0:1] + acc[512:1024] * rows[1:2]
    comb[...] = mixed.reshape(Y, CORES, PIECE, RANK)
    send(comb.at[:, 1 - c], ccore, mc_send, mc_recv, peer)

    arrived(cbuf.at[1 - c], c_recv)
    arrived(gall.at[1 - c], gp_recv)
    factor = cbuf[...].reshape(16, RANK).astype(jnp.bfloat16)
    n = gall[...].reshape(RANK, RANK) * lax.dot_general(
        factor, factor, (((0,), (0,)), ((), ())), preferred_element_type=jnp.float32
    )
    eye = lax.broadcasted_iota(jnp.int32, n.shape, 0) == lax.broadcasted_iota(jnp.int32, n.shape, 1)
    diag = jnp.where(eye, n, 0.0)
    sr = lax.rsqrt(jnp.sum(diag, axis=0, keepdims=True))
    sc = lax.rsqrt(jnp.sum(diag, axis=1, keepdims=True))
    matrix[...] = n * sr * sc

    def hook(panel):
        if panel != 3:
            return

        @pl.when(ia >= 0)
        def _():
            arrived(ccore, mc_recv)
            csum[...] = ccore[...] + comb[:, c]
            for dy in (1, 3, 2):
                send(csum.at[lax.rem(y + dy, Y)], my.at[y], my_send, my_recv, at(dy=dy))
            my[y] = csum[y]

    invert(matrix, hook)
    arrived(my.at[0:3], my_recv)
    m = jnp.sum(my[...], axis=0) * sr
    out_ref[0] = -dot(m, matrix[...]) * sr

    sent(bbuf.at[z, :, c], o_send)
    sent(bbuf.at[0:7, 0, c], z_send)
    for dz in range(Z):
        sent(group(dz), g_send.at[dz])
    sent(bbuf.at[0:7, :, c], k_send)
    sent(cbuf.at[c], c_send)
    sent(gxy.at[0:15], gxy_send)
    sent(gz.at[0:7], gz_send)
    sent(gxy.at[0:15], ga_send)
    sent(gall.at[c], gp_send)
    sent(ccore, mc_send)
    sent(my.at[0:3], my_send)


def per_device(tensor, factor_b, factor_c):
    f32, bf16 = jnp.float32, jnp.bfloat16
    vmem = pl.BlockSpec(memory_space=pltpu.VMEM)
    hbm = pl.BlockSpec(memory_space=pl.ANY)
    dma = pltpu.SemaphoreType.DMA
    return pl.pallas_call(
        als_kernel,
        out_shape=jax.ShapeDtypeStruct((1, PIECE, RANK), f32),
        in_specs=[hbm, hbm, vmem],
        out_specs=vmem,
        scratch_shapes=[
            pltpu.VMEM((Z, 2, 512, 512), bf16),
            pltpu.VMEM((Z, X, CORES, PIECE, RANK), bf16),
            pltpu.VMEM((1024, RANK), f32),
            pltpu.VMEM((CORES, 8, RANK), f32),
            pltpu.VMEM((16, 8, RANK), f32),
            pltpu.VMEM((16, 8, RANK), f32),
            pltpu.VMEM((Z, 8, RANK), f32),
            pltpu.VMEM((8, RANK), f32),
            pltpu.VMEM((CORES, 16, 8, RANK), f32),
            pltpu.VMEM((Y, CORES, PIECE, RANK), f32),
            pltpu.VMEM((Y, PIECE, RANK), f32),
            pltpu.VMEM((Y, PIECE, RANK), f32),
            pltpu.VMEM((Y, PIECE, RANK), f32),
            pltpu.VMEM((RANK, RANK), f32),
            dma((Z,)), dma, dma, dma((Z,)), dma((Z,)), dma((Z,)), dma, dma((Z,)), dma, dma, dma, dma,
            dma, dma, dma, dma, dma, dma, dma, dma, dma, dma, dma, dma,
        ],
        compiler_params=pltpu.CompilerParams(
            collective_id=0, has_side_effects=True, vmem_limit_bytes=48 * 2**20
        ),
        cost_estimate=pl.CostEstimate(flops=2**31, bytes_accessed=2**23, transcendentals=0),
        name="als",
    )(tensor, factor_b, factor_c)


def solution(mesh):
    return jax.shard_map(
        per_device,
        mesh=mesh,
        in_specs=(P("ka", "ia", "ja"), P("ja", ("ia", "ka"), None), P("ka", None, None)),
        out_specs=P("ia", ("ja", "ka"), None),
        check_vma=False,
    )
```

```python
import jax, jax.numpy as jnp
from jax import lax
from jax.experimental import pallas as pl
from jax.experimental.pallas import tpu as pltpu
from jax.sharding import PartitionSpec as P
HI=lax.Precision.HIGHEST


def dot(a,b,ta=False,tb=False):
    return lax.dot_general(a,b,(((0 if ta else 1,),(1 if tb else 0,)),((),())),precision=HI,preferred_element_type=jnp.float32)


def split(v):
    hi = v.astype(jnp.bfloat16)
    rest = v - hi.astype(jnp.float32)
    mid = rest.astype(jnp.bfloat16)
    return hi, mid, (rest - mid.astype(jnp.float32)).astype(jnp.bfloat16)


def invert(aref, hook=None):
    lane = lax.broadcasted_iota(jnp.int32, (8, 128), 1)
    sub = lax.broadcasted_iota(jnp.int32, (8, 128), 0)

    def read(row):
        return [aref[row : row + 8, 0:128], aref[row : row + 8, 128:256]]

    def over_lanes(tile, k):
        v = tile[k // 128]
        return jnp.broadcast_to(v[:, k % 128 : k % 128 + 1], (8, 128))

    def over_rows(v, i):
        return jnp.broadcast_to(v[i : i + 1, :], (8, 128))

    def eliminate(tile, first, done):
        count = 8 * len(done)
        half, off = first // 128, first % 128
        spread = [over_lanes(tile, first + m) for m in range(count)]
        new = []
        for side in range(2):
            parts = [spread[m] * over_rows(done[m // 8][side], m % 8) for m in range(count)]
            while len(parts) > 1:
                parts = [parts[i] + parts[i + 1] for i in range(0, len(parts), 2)]
            kept = tile[side]
            if side == half:
                kept = jnp.where((lane >= off) & (lane < off + count), 0.0, kept)
            new.append(kept - parts[0])
        return new

    tiles = [read(0), read(8)]
    for panel in range(16):
        if hook is not None:
            hook(panel)
        base = 16 * panel
        half, off = base // 128, base % 128
        for h in range(2):
            cols = [over_lanes(tiles[h], base + 8 * h + m) for m in range(8)]
            for s in range(4):
                i0, i1 = 2 * s, 2 * s + 1
                k0, k1 = base + 8 * h + i0, base + 8 * h + i1
                c0, c1 = cols[i0], cols[i1]
                a, b, d = over_rows(c0, i0), over_rows(c1, i0), over_rows(c1, i1)
                r = 1.0 / (a * d - b * b)
                at0, at1 = lane == k0 % 128, lane == k1 % 128
                either = at0 | at1
                rows = (sub == i0) | (sub == i1)
                e0 = jnp.where(sub == i0, -1.0, jnp.where(sub == i1, 0.0, c0))
                e1 = jnp.where(sub == i1, -1.0, jnp.where(sub == i0, 0.0, c1))
                for m in range(i1 + 1, 8):
                    t0, t1 = over_rows(cols[m], i0), over_rows(cols[m], i1)
                    g = e0 * (d * t0 - b * t1) + e1 * (a * t1 - b * t0)
                    cols[m] = jnp.where(rows, 0.0, cols[m]) - g * r
                mine = []
                for side in range(2):
                    T = tiles[h][side]
                    row0, row1 = over_rows(T, i0), over_rows(T, i1)
                    w0, w1 = d * row0 - b * row1, a * row1 - b * row0
                    T = jnp.where(rows, 0.0, T)
                    if side == half:
                        w0 = jnp.where(at0, -d, jnp.where(at1, b, w0))
                        w1 = jnp.where(at0, b, jnp.where(at1, -a, w1))
                        T = jnp.where(either, 0.0, T)
                    w0, w1 = w0 * r, w1 * r
                    mine.append(T - e0 * w0 - e1 * w1)
                tiles[h] = mine
            tiles[1 - h] = eliminate(tiles[1 - h], base + 8 * h, [tiles[h]])
        done = tiles
        if panel < 15:
            tiles = [eliminate(read(base + 16 + 8 * q), base, done) for q in range(2)]
        w = jnp.concatenate([jnp.concatenate(t, axis=1) for t in done], axis=0)
        wh, wm, wl = split(w)

        def pad(v):
            parts = [v]
            if off:
                parts.insert(0, jnp.zeros((off, 256), jnp.bfloat16))
            if off < 112:
                parts.append(jnp.zeros((112 - off, 256), jnp.bfloat16))
            return jnp.concatenate(parts, axis=0) if len(parts) > 1 else v

        hi, mid, lo = split(aref[:, 128 * half : 128 * half + 128])
        both = jnp.concatenate([hi, mid], axis=1)
        f = lambda l, r0, r1: jnp.dot(l, jnp.concatenate([pad(r0), pad(r1)], axis=0), preferred_element_type=jnp.float32)
        change = f(both, wh, wh) + f(both, wm, wm) + f(jnp.concatenate([hi, lo], axis=1), wl, wh)
        lanes = lax.broadcasted_iota(jnp.int32, (256, 256), 1)
        keep = jnp.where((lanes >= base) & (lanes < base + 16), 0.0, aref[...])
        aref[...] = keep - change
        aref[base : base + 16, :] = w


Z, X, Y, CORES = 8, 4, 4, 2
PIECE = 64
RANK = 256
MESH = pl.DeviceIdType.MESH


def distance(step):
    return lax.rem(step, 2) * ((step + 1) // 2) + (1 - lax.rem(step, 2)) * lax.rem(Z - step // 2, Z)


def als_kernel(
    x_hbm, b_hbm, c_ref, out_ref,
    xbuf, bbuf, acc, cbuf, gpart, gxy, gz, gslice, gall, comb, ccore, csum, my, matrix,
    x_sem, b_sem, z_send, z_recv, g_send, g_recv, k_send, k_recv, o_send, o_recv, c_send, c_recv,
    gxy_send, gxy_recv, gz_send, gz_recv, ga_send, ga_recv, gp_send, gp_recv,
    mc_send, mc_recv, my_send, my_recv,
):
    ia, y, c = lax.axis_index("ia"), lax.axis_index("ja"), lax.axis_index("ka")
    z, x = ia // X, lax.rem(ia, X)
    peer = (ia, y, 1 - c)
    slot = y * X + x

    def at(dz=0, dx=0, dy=0):
        zz, xx = lax.rem(z + dz, Z), lax.rem(x + dx, X)
        return (zz * X + xx, lax.rem(y + dy, Y), c)

    def send(src, dst, ss, rs, to):
        copy = pltpu.make_async_remote_copy(
            src_ref=src, dst_ref=dst, send_sem=ss, recv_sem=rs, device_id=to, device_id_type=MESH
        )
        copy.start()

    def arrived(ref, sem):
        pltpu.make_async_remote_copy(
            src_ref=ref, dst_ref=ref, send_sem=sem, recv_sem=sem, device_id=peer, device_id_type=MESH
        ).wait_recv()

    def sent(ref, sem):
        pltpu.make_async_remote_copy(
            src_ref=ref, dst_ref=ref, send_sem=sem, recv_sem=sem, device_id=peer, device_id_type=MESH
        ).wait_send()

    def load(step):
        zz = lax.rem(z + distance(step), Z)
        return pltpu.make_async_copy(
            x_hbm.at[:, :, pl.ds(pl.multiple_of(zz * 512, 512), 512)], xbuf.at[zz], x_sem.at[step]
        )

    plane = [(dx, dy) for dy in (2, 1, 3, 0) for dx in (2, 1, 3, 0) if dx or dy]
    partners = [at(dz=d) for d in range(1, Z)] + [at(dx=dx, dy=dy) for dx, dy in plane] + [peer]
    barrier = pltpu.get_barrier_semaphore()
    for to in partners:
        pl.semaphore_signal(barrier, inc=1, device_id=to, device_id_type=MESH)
    own = bbuf.at[z, x, c]
    own_load = pltpu.make_async_copy(b_hbm.at[0], own, b_sem)
    own_load.start()
    for step in range(Z):
        load(jnp.int32(step)).start()
    cbuf[c] = jnp.concatenate([c_ref[0].astype(jnp.float32), jnp.zeros((6, RANK), jnp.float32)], axis=0)
    acc[...] = jnp.zeros_like(acc)
    own_load.wait()
    pl.semaphore_wait(barrier, len(partners))

    send(own, own, o_send, o_recv, peer)
    for dz in (1, 7, 2, 6, 3, 5, 4):
        send(own, own, z_send, z_recv.at[Z - dz], at(dz=dz))
    send(cbuf.at[c], cbuf.at[c], c_send, c_recv, peer)

    arrived(bbuf.at[z, x, 1 - c], o_recv)
    mine = bbuf[z, x, :, :, pl.ds(pl.multiple_of(c * 128, 128), 128)].reshape(128, 128)
    gpart[...] = lax.dot_general(
        mine, bbuf[z, x].reshape(128, RANK), (((0,), (0,)), ((), ())), preferred_element_type=jnp.float32
    ).reshape(16, 8, RANK)
    for dx, dy in plane:
        target = lax.rem(y + dy, Y) * X + lax.rem(x + dx, X)
        send(gpart.at[target], gxy.at[slot], gxy_send, gxy_recv, at(dx=dx, dy=dy))
    for dx in (1, 3, 2):
        send(own, own, g_send.at[0], g_recv.at[0], at(dx=dx))
    gxy[slot] = gpart[slot]

    def group(dz):
        return bbuf.at[lax.rem(z + dz, Z), 0:3, c]

    def relay(step, _):
        dz = distance(step)
        zz = lax.rem(z + dz, Z)
        piece = bbuf.at[zz, x, c]
        arrived(piece, z_recv.at[dz])
        send(piece, piece, g_send.at[dz], g_recv.at[dz], at(dx=1))
        send(piece, piece, g_send.at[dz], g_recv.at[dz], at(dx=3))
        half = bbuf.at[zz, x, c, 0:32]
        send(half, half, g_send.at[dz], g_recv.at[dz], at(dx=2))
        return 0

    lax.fori_loop(1, 3, relay, 0)
    arrived(gxy.at[0:15], gxy_recv)
    gz[z] = jnp.sum(gxy[...], axis=0)
    for dz in (4, 3, 5, 2, 6, 1, 7):
        send(gz.at[z], gz.at[z], gz_send, gz_recv, at(dz=dz))
    arrived(group(0), g_recv.at[0])
    half = bbuf.at[z, lax.rem(x + 2, X), c, 32:64]
    for dz in (1, 7, 2, 6, 3, 5, 4):
        send(half, half, g_send.at[dz], g_recv.at[Z - dz], at(dz=dz))
    for dx in (1, 3, 2):
        part = bbuf.at[z, lax.rem(x + dx, X), c]
        send(part, part, o_send, k_recv.at[0], peer)

    lax.fori_loop(3, Z, relay, 0)

    def gram_over_plane():
        arrived(gz.at[0:7], gz_recv)
        gslice[...] = jnp.sum(gz[...], axis=0)
        for dx, dy in plane:
            send(gslice, gall.at[c, slot], ga_send, ga_recv, at(dx=dx, dy=dy))
        gall[c, slot] = gslice[...]

    def gram_to_peer():
        arrived(gall.at[c, 0:15], ga_recv)
        send(gall.at[c], gall.at[c], gp_send, gp_recv, peer)

    def chunk(step, _):
        dz = distance(step)
        zz = lax.rem(z + dz, Z)

        @pl.when(step < Z - 1)
        def _():
            later = distance(step + 1)
            arrived(group(later), g_recv.at[later])
            part = bbuf.at[lax.rem(z + later, Z), :, c]
            send(part, part, k_send, k_recv.at[later], peer)

        @pl.when(step == 7)
        def _():
            gram_to_peer()

        @pl.when(step == 0)
        def _():
            arrived(bbuf.at[z, 0:3, 1 - c], k_recv.at[0])

        @pl.when(step > 0)
        def _():
            arrived(bbuf.at[zz, :, 1 - c], k_recv.at[dz])

        load(step).wait()
        acc[...] += jnp.dot(
            xbuf[zz].reshape(1024, 512), bbuf[zz].reshape(512, RANK), preferred_element_type=jnp.float32
        )
        return 0

    gram_over_plane()
    lax.fori_loop(0, Z, chunk, 0)
    rows = c_ref[0].astype(jnp.float32)
    mixed = acc[0:512] * rows[0:1] + acc[512:1024] * rows[1:2]
    comb[...] = mixed.reshape(Y, CORES, PIECE, RANK)
    send(comb.at[:, 1 - c], ccore, mc_send, mc_recv, peer)

    arrived(cbuf.at[1 - c], c_recv)
    arrived(gall.at[1 - c], gp_recv)
    factor = cbuf[...].reshape(16, RANK).astype(jnp.bfloat16)
    n = gall[...].reshape(RANK, RANK) * lax.dot_general(
        factor, factor, (((0,), (0,)), ((), ())), preferred_element_type=jnp.float32
    )
    eye = lax.broadcasted_iota(jnp.int32, n.shape, 0) == lax.broadcasted_iota(jnp.int32, n.shape, 1)
    diag = jnp.where(eye, n, 0.0)
    sr = lax.rsqrt(jnp.sum(diag, axis=0, keepdims=True))
    sc = lax.rsqrt(jnp.sum(diag, axis=1, keepdims=True))
    matrix[...] = n * sr * sc

    def hook(panel):
        if panel != 3:
            return

        @pl.when(ia >= 0)
        def _():
            arrived(ccore, mc_recv)
            csum[...] = ccore[...] + comb[:, c]
            for dy in (1, 3, 2):
                send(csum.at[lax.rem(y + dy, Y)], my.at[y], my_send, my_recv, at(dy=dy))
            my[y] = csum[y]

    invert(matrix, hook)
    arrived(my.at[0:3], my_recv)
    m = jnp.sum(my[...], axis=0) * sr
    out_ref[0] = -dot(m, matrix[...]) * sr

    sent(bbuf.at[z, :, c], o_send)
    sent(bbuf.at[0:7, 0, c], z_send)
    for dz in range(Z):
        sent(group(dz), g_send.at[dz])
    sent(bbuf.at[0:7, :, c], k_send)
    sent(cbuf.at[c], c_send)
    sent(gxy.at[0:15], gxy_send)
    sent(gz.at[0:7], gz_send)
    sent(gxy.at[0:15], ga_send)
    sent(gall.at[c], gp_send)
    sent(ccore, mc_send)
    sent(my.at[0:3], my_send)


def per_device(tensor, factor_b, factor_c):
    f32, bf16 = jnp.float32, jnp.bfloat16
    vmem = pl.BlockSpec(memory_space=pltpu.VMEM)
    hbm = pl.BlockSpec(memory_space=pl.ANY)
    dma = pltpu.SemaphoreType.DMA
    return pl.pallas_call(
        als_kernel,
        out_shape=jax.ShapeDtypeStruct((1, PIECE, RANK), f32),
        in_specs=[hbm, hbm, vmem],
        out_specs=vmem,
        scratch_shapes=[
            pltpu.VMEM((Z, 2, 512, 512), bf16),
            pltpu.VMEM((Z, X, CORES, PIECE, RANK), bf16),
            pltpu.VMEM((1024, RANK), f32),
            pltpu.VMEM((CORES, 8, RANK), f32),
            pltpu.VMEM((16, 8, RANK), f32),
            pltpu.VMEM((16, 8, RANK), f32),
            pltpu.VMEM((Z, 8, RANK), f32),
            pltpu.VMEM((8, RANK), f32),
            pltpu.VMEM((CORES, 16, 8, RANK), f32),
            pltpu.VMEM((Y, CORES, PIECE, RANK), f32),
            pltpu.VMEM((Y, PIECE, RANK), f32),
            pltpu.VMEM((Y, PIECE, RANK), f32),
            pltpu.VMEM((Y, PIECE, RANK), f32),
            pltpu.VMEM((RANK, RANK), f32),
            dma((Z,)), dma, dma, dma((Z,)), dma((Z,)), dma((Z,)), dma, dma((Z,)), dma, dma, dma, dma,
            dma, dma, dma, dma, dma, dma, dma, dma, dma, dma, dma, dma,
        ],
        compiler_params=pltpu.CompilerParams(
            collective_id=0, has_side_effects=True, vmem_limit_bytes=48 * 2**20
        ),
        cost_estimate=pl.CostEstimate(flops=2**31, bytes_accessed=2**23, transcendentals=0),
        name="als",
    )(tensor, factor_b, factor_c)


def solution(mesh):
    return jax.shard_map(
        per_device,
        mesh=mesh,
        in_specs=(P("ka", "ia", "ja"), P("ja", ("ia", "ka"), None), P("ka", None, None)),
        out_specs=P("ia", ("ja", "ka"), None),
        check_vma=False,
    )
```

```python
import jax, jax.numpy as jnp
from jax import lax
from jax.experimental import pallas as pl
from jax.experimental.pallas import tpu as pltpu
from jax.sharding import PartitionSpec as P
HI=lax.Precision.HIGHEST


def dot(a,b,ta=False,tb=False):
    return lax.dot_general(a,b,(((0 if ta else 1,),(1 if tb else 0,)),((),())),precision=HI,preferred_element_type=jnp.float32)


NEAR = 3


def split(v):
    hi = v.astype(jnp.bfloat16)
    rest = v - hi.astype(jnp.float32)
    mid = rest.astype(jnp.bfloat16)
    return hi, mid, (rest - mid.astype(jnp.float32)).astype(jnp.bfloat16)


def invert(aref, hook=None):
    lane = lax.broadcasted_iota(jnp.int32, (8, 128), 1)
    sub = lax.broadcasted_iota(jnp.int32, (8, 128), 0)

    def read(row):
        return [aref[row : row + 8, 0:128], aref[row : row + 8, 128:256]]

    def over_lanes(tile, k):
        v = tile[k // 128]
        return jnp.broadcast_to(v[:, k % 128 : k % 128 + 1], (8, 128))

    def over_rows(v, i):
        return jnp.broadcast_to(v[i : i + 1, :], (8, 128))

    def eliminate(tile, first, done):
        count = 8 * len(done)
        half, off = first // 128, first % 128
        spread = [over_lanes(tile, first + m) for m in range(count)]
        new = []
        for side in range(2):
            parts = [spread[m] * over_rows(done[m // 8][side], m % 8) for m in range(count)]
            while len(parts) > 1:
                parts = [parts[i] + parts[i + 1] for i in range(0, len(parts), 2)]
            kept = tile[side]
            if side == half:
                kept = jnp.where((lane >= off) & (lane < off + count), 0.0, kept)
            new.append(kept - parts[0])
        return new

    tiles = [read(0), read(8)]
    for panel in range(16):
        if hook is not None:
            hook(panel)
        base = 16 * panel
        half, off = base // 128, base % 128
        for h in range(2):
            cols = [over_lanes(tiles[h], base + 8 * h + m) for m in range(8)]
            for s in range(4):
                i0, i1 = 2 * s, 2 * s + 1
                k0, k1 = base + 8 * h + i0, base + 8 * h + i1
                c0, c1 = cols[i0], cols[i1]
                a, b, d = over_rows(c0, i0), over_rows(c1, i0), over_rows(c1, i1)
                r = 1.0 / (a * d - b * b)
                at0, at1 = lane == k0 % 128, lane == k1 % 128
                either = at0 | at1
                rows = (sub == i0) | (sub == i1)
                e0 = jnp.where(sub == i0, -1.0, jnp.where(sub == i1, 0.0, c0))
                e1 = jnp.where(sub == i1, -1.0, jnp.where(sub == i0, 0.0, c1))
                q0, q1 = (d * e0 - b * e1) * r, (a * e1 - b * e0) * r
                for m in range(i1 + 1, 8):
                    t0, t1 = over_rows(cols[m], i0), over_rows(cols[m], i1)
                    kept = jnp.where(rows, 0.0, cols[m])
                    if m < i1 + NEAR:
                        g = e0 * (d * t0 - b * t1) + e1 * (a * t1 - b * t0)
                        cols[m] = kept - g * r
                    else:
                        cols[m] = kept - (q0 * t0 + q1 * t1)
                mine = []
                for side in range(2):
                    T = tiles[h][side]
                    row0, row1 = over_rows(T, i0), over_rows(T, i1)
                    T = jnp.where(rows, 0.0, T)
                    if side == half:
                        row0 = jnp.where(at0, -1.0, jnp.where(at1, 0.0, row0))
                        row1 = jnp.where(at1, -1.0, jnp.where(at0, 0.0, row1))
                        T = jnp.where(either, 0.0, T)
                    mine.append(T - (q0 * row0 + q1 * row1))
                tiles[h] = mine
            tiles[1 - h] = eliminate(tiles[1 - h], base + 8 * h, [tiles[h]])
        done = tiles
        if panel < 15:
            tiles = [eliminate(read(base + 16 + 8 * q), base, done) for q in range(2)]
        w = jnp.concatenate([jnp.concatenate(t, axis=1) for t in done], axis=0)
        wh, wm, wl = split(w)

        def pad(v):
            parts = [v]
            if off:
                parts.insert(0, jnp.zeros((off, 256), jnp.bfloat16))
            if off < 112:
                parts.append(jnp.zeros((112 - off, 256), jnp.bfloat16))
            return jnp.concatenate(parts, axis=0) if len(parts) > 1 else v

        hi, mid, lo = split(aref[:, 128 * half : 128 * half + 128])
        change = jnp.dot(
            jnp.concatenate([hi, mid, hi, mid, hi, lo], axis=1),
            jnp.concatenate([pad(v) for v in (wh, wh, wm, wm, wl, wh)], axis=0),
            preferred_element_type=jnp.float32,
        )
        lanes = lax.broadcasted_iota(jnp.int32, (256, 128), 1)
        inside = (lanes >= off) & (lanes < off + 16)
        for side in range(2):
            span = slice(128 * side, 128 * side + 128)
            kept = aref[:, span]
            if side == half:
                kept = jnp.where(inside, 0.0, kept)
            aref[:, span] = kept - change[:, span]
        aref[base : base + 16, :] = w


Z, X, Y, CORES = 8, 4, 4, 2
PIECE = 64
RANK = 256
MESH = pl.DeviceIdType.MESH


def distance(step):
    return lax.rem(step, 2) * ((step + 1) // 2) + (1 - lax.rem(step, 2)) * lax.rem(Z - step // 2, Z)


def als_kernel(
    x_hbm, b_hbm, c_ref, out_ref,
    xbuf, bbuf, acc, cbuf, gpart, gxy, gz, gslice, gall, comb, ccore, csum, my, matrix,
    x_sem, b_sem, z_send, z_recv, g_send, g_recv, k_send, k_recv, o_send, o_recv, c_send, c_recv,
    gxy_send, gxy_recv, gz_send, gz_recv, ga_send, ga_recv, gp_send, gp_recv,
    mc_send, mc_recv, my_send, my_recv,
):
    ia, y, c = lax.axis_index("ia"), lax.axis_index("ja"), lax.axis_index("ka")
    z, x = ia // X, lax.rem(ia, X)
    peer = (ia, y, 1 - c)
    slot = y * X + x

    def at(dz=0, dx=0, dy=0):
        zz, xx = lax.rem(z + dz, Z), lax.rem(x + dx, X)
        return (zz * X + xx, lax.rem(y + dy, Y), c)

    def send(src, dst, ss, rs, to):
        copy = pltpu.make_async_remote_copy(
            src_ref=src, dst_ref=dst, send_sem=ss, recv_sem=rs, device_id=to, device_id_type=MESH
        )
        copy.start()

    def arrived(ref, sem):
        pltpu.make_async_remote_copy(
            src_ref=ref, dst_ref=ref, send_sem=sem, recv_sem=sem, device_id=peer, device_id_type=MESH
        ).wait_recv()

    def sent(ref, sem):
        pltpu.make_async_remote_copy(
            src_ref=ref, dst_ref=ref, send_sem=sem, recv_sem=sem, device_id=peer, device_id_type=MESH
        ).wait_send()

    def load(step):
        zz = lax.rem(z + distance(step), Z)
        return pltpu.make_async_copy(
            x_hbm.at[:, :, pl.ds(pl.multiple_of(zz * 512, 512), 512)], xbuf.at[zz], x_sem.at[step]
        )

    plane = [(dx, dy) for dy in (2, 1, 3, 0) for dx in (2, 1, 3, 0) if dx or dy]
    partners = [at(dz=d) for d in range(1, Z)] + [at(dx=dx, dy=dy) for dx, dy in plane] + [peer]
    barrier = pltpu.get_barrier_semaphore()
    for to in partners:
        pl.semaphore_signal(barrier, inc=1, device_id=to, device_id_type=MESH)
    own = bbuf.at[z, x, c]
    own_load = pltpu.make_async_copy(b_hbm.at[0], own, b_sem)
    own_load.start()
    for step in range(Z):
        load(jnp.int32(step)).start()
    cbuf[c] = jnp.concatenate([c_ref[0].astype(jnp.float32), jnp.zeros((6, RANK), jnp.float32)], axis=0)
    acc[...] = jnp.zeros_like(acc)
    own_load.wait()
    pl.semaphore_wait(barrier, len(partners))

    send(own, own, o_send, o_recv, peer)
    for dz in (1, 7, 2, 6, 3, 5, 4):
        send(own, own, z_send, z_recv.at[Z - dz], at(dz=dz))
    send(cbuf.at[c], cbuf.at[c], c_send, c_recv, peer)

    arrived(bbuf.at[z, x, 1 - c], o_recv)
    mine = bbuf[z, x, :, :, pl.ds(pl.multiple_of(c * 128, 128), 128)].reshape(128, 128)
    gpart[...] = lax.dot_general(
        mine, bbuf[z, x].reshape(128, RANK), (((0,), (0,)), ((), ())), preferred_element_type=jnp.float32
    ).reshape(16, 8, RANK)
    for dx, dy in plane:
        target = lax.rem(y + dy, Y) * X + lax.rem(x + dx, X)
        send(gpart.at[target], gxy.at[slot], gxy_send, gxy_recv, at(dx=dx, dy=dy))
    for dx in (1, 3, 2):
        send(own, own, g_send.at[0], g_recv.at[0], at(dx=dx))
    gxy[slot] = gpart[slot]

    def group(dz):
        return bbuf.at[lax.rem(z + dz, Z), 0:3, c]

    def relay(step, _):
        dz = distance(step)
        zz = lax.rem(z + dz, Z)
        piece = bbuf.at[zz, x, c]
        arrived(piece, z_recv.at[dz])
        send(piece, piece, g_send.at[dz], g_recv.at[dz], at(dx=1))
        send(piece, piece, g_send.at[dz], g_recv.at[dz], at(dx=3))
        half = bbuf.at[zz, x, c, 0:32]
        send(half, half, g_send.at[dz], g_recv.at[dz], at(dx=2))
        return 0

    lax.fori_loop(1, 3, relay, 0)
    arrived(gxy.at[0:15], gxy_recv)
    gz[z] = jnp.sum(gxy[...], axis=0)
    for dz in (4, 3, 5, 2, 6, 1, 7):
        send(gz.at[z], gz.at[z], gz_send, gz_recv, at(dz=dz))
    arrived(group(0), g_recv.at[0])
    half = bbuf.at[z, lax.rem(x + 2, X), c, 32:64]
    for dz in (1, 7, 2, 6, 3, 5, 4):
        send(half, half, g_send.at[dz], g_recv.at[Z - dz], at(dz=dz))
    for dx in (1, 3, 2):
        part = bbuf.at[z, lax.rem(x + dx, X), c]
        send(part, part, o_send, k_recv.at[0], peer)

    lax.fori_loop(3, Z, relay, 0)

    def gram_over_plane():
        arrived(gz.at[0:7], gz_recv)
        gslice[...] = jnp.sum(gz[...], axis=0)
        for dx, dy in plane:
            send(gslice, gall.at[c, slot], ga_send, ga_recv, at(dx=dx, dy=dy))
        gall[c, slot] = gslice[...]

    def gram_to_peer():
        arrived(gall.at[c, 0:15], ga_recv)
        send(gall.at[c], gall.at[c], gp_send, gp_recv, peer)

    def chunk(step, _):
        dz = distance(step)
        zz = lax.rem(z + dz, Z)

        @pl.when(step < Z - 1)
        def _():
            later = distance(step + 1)
            arrived(group(later), g_recv.at[later])
            part = bbuf.at[lax.rem(z + later, Z), :, c]
            send(part, part, k_send, k_recv.at[later], peer)

        @pl.when(step == 7)
        def _():
            gram_to_peer()

        @pl.when(step == 0)
        def _():
            arrived(bbuf.at[z, 0:3, 1 - c], k_recv.at[0])

        @pl.when(step > 0)
        def _():
            arrived(bbuf.at[zz, :, 1 - c], k_recv.at[dz])

        load(step).wait()
        acc[...] += jnp.dot(
            xbuf[zz].reshape(1024, 512), bbuf[zz].reshape(512, RANK), preferred_element_type=jnp.float32
        )
        return 0

    gram_over_plane()
    lax.fori_loop(0, Z, chunk, 0)
    rows = c_ref[0].astype(jnp.float32)
    mixed = acc[0:512] * rows[0:1] + acc[512:1024] * rows[1:2]
    comb[...] = mixed.reshape(Y, CORES, PIECE, RANK)
    send(comb.at[:, 1 - c], ccore, mc_send, mc_recv, peer)

    arrived(cbuf.at[1 - c], c_recv)
    factor = cbuf[...].reshape(16, RANK).astype(jnp.bfloat16)
    matrix[...] = lax.dot_general(
        factor, factor, (((0,), (0,)), ((), ())), preferred_element_type=jnp.float32
    )
    arrived(gall.at[1 - c], gp_recv)
    n = gall[...].reshape(RANK, RANK) * matrix[...]
    eye = lax.broadcasted_iota(jnp.int32, n.shape, 0) == lax.broadcasted_iota(jnp.int32, n.shape, 1)
    diag = jnp.where(eye, n, 0.0)
    sr = lax.rsqrt(jnp.sum(diag, axis=0, keepdims=True))
    sc = lax.rsqrt(jnp.sum(diag, axis=1, keepdims=True))
    matrix[...] = n * sr * sc

    def hook(panel):
        if panel != 1:
            return

        @pl.when(ia >= 0)
        def _():
            arrived(ccore, mc_recv)
            csum[...] = ccore[...] + comb[:, c]
            for dy in (1, 3, 2):
                send(csum.at[lax.rem(y + dy, Y)], my.at[y], my_send, my_recv, at(dy=dy))
            my[y] = csum[y]

    invert(matrix, hook)
    arrived(my.at[0:3], my_recv)
    m = jnp.sum(my[...], axis=0) * sr
    out_ref[0] = -dot(m, matrix[...]) * sr

    sent(bbuf.at[z, :, c], o_send)
    sent(bbuf.at[0:7, 0, c], z_send)
    for dz in range(Z):
        sent(group(dz), g_send.at[dz])
    sent(bbuf.at[0:7, :, c], k_send)
    sent(cbuf.at[c], c_send)
    sent(gxy.at[0:15], gxy_send)
    sent(gz.at[0:7], gz_send)
    sent(gxy.at[0:15], ga_send)
    sent(gall.at[c], gp_send)
    sent(ccore, mc_send)
    sent(my.at[0:3], my_send)


def per_device(tensor, factor_b, factor_c):
    f32, bf16 = jnp.float32, jnp.bfloat16
    vmem = pl.BlockSpec(memory_space=pltpu.VMEM)
    hbm = pl.BlockSpec(memory_space=pl.ANY)
    dma = pltpu.SemaphoreType.DMA
    return pl.pallas_call(
        als_kernel,
        out_shape=jax.ShapeDtypeStruct((1, PIECE, RANK), f32),
        in_specs=[hbm, hbm, vmem],
        out_specs=vmem,
        scratch_shapes=[
            pltpu.VMEM((Z, 2, 512, 512), bf16),
            pltpu.VMEM((Z, X, CORES, PIECE, RANK), bf16),
            pltpu.VMEM((1024, RANK), f32),
            pltpu.VMEM((CORES, 8, RANK), f32),
            pltpu.VMEM((16, 8, RANK), f32),
            pltpu.VMEM((16, 8, RANK), f32),
            pltpu.VMEM((Z, 8, RANK), f32),
            pltpu.VMEM((8, RANK), f32),
            pltpu.VMEM((CORES, 16, 8, RANK), f32),
            pltpu.VMEM((Y, CORES, PIECE, RANK), f32),
            pltpu.VMEM((Y, PIECE, RANK), f32),
            pltpu.VMEM((Y, PIECE, RANK), f32),
            pltpu.VMEM((Y, PIECE, RANK), f32),
            pltpu.VMEM((RANK, RANK), f32),
            dma((Z,)), dma, dma, dma((Z,)), dma((Z,)), dma((Z,)), dma, dma((Z,)), dma, dma, dma, dma,
            dma, dma, dma, dma, dma, dma, dma, dma, dma, dma, dma, dma,
        ],
        compiler_params=pltpu.CompilerParams(
            collective_id=0, has_side_effects=True, vmem_limit_bytes=48 * 2**20
        ),
        cost_estimate=pl.CostEstimate(flops=2**31, bytes_accessed=2**23, transcendentals=0),
        name="als",
    )(tensor, factor_b, factor_c)


def solution(mesh):
    return jax.shard_map(
        per_device,
        mesh=mesh,
        in_specs=(P("ka", "ia", "ja"), P("ja", ("ia", "ka"), None), P("ka", None, None)),
        out_specs=P("ia", ("ja", "ka"), None),
        check_vma=False,
    )
```
